256 devices in a mesh: segment: 8 (over z), dp: 32 (over x, y, core).
Axes of the slice: x: 4, y: 4, z: 8, core: 2. Of those that a mesh axis runs over, the one named last changes fastest.
Arguments:
- arriving: float32 [8, 32, 128, 1024], P('segment', 'dp'), may hold values from -6 to 6
- entering: float32 [1, 32, 128, 1024], P(None, 'dp'), may hold values from -6 to 6
- returning: float32 [8, 32, 128, 1024], P('segment', 'dp'), may hold values from -6 to 6
- loss_grad: float32 [1, 32, 128, 1024], P(None, 'dp'), may hold values from -6 to 6
- kept: float32 [8, 3, 32, 128, 1024], P('segment', None, 'dp'), may hold values from -6 to 6
- lent: float32 [8, 3, 32, 128, 1024], P('segment', None, 'dp'), may hold values from -6 to 6
- w_in: float32 [8, 1024, 2048], P('segment', 'dp'), may hold values from -0.1875 to 0.1875
- kernel: float32 [8, 31, 1024], P('segment'), may hold values from -1 to 1
- w_out: float32 [8, 1024, 1024], P('segment', 'dp'), may hold values from -0.1875 to 0.1875
- evict: int32 [8, 2], replicated, may hold values from 0 to 5, as said below
- recall: int32 [8, 2], replicated, may hold values from 0 to 5, as said below
Outputs:
- passed: float32 [8, 32, 128, 1024], P('segment', 'dp')
- returned: float32 [8, 32, 128, 1024], P('segment', 'dp')
- kept_out: float32 [8, 3, 32, 128, 1024], P('segment', None, 'dp')
- lent_out: float32 [8, 3, 32, 128, 1024], P('segment', None, 'dp')
- grad_in: float32 [8, 1024, 2048], P('segment', 'dp')
- grad_kernel: float32 [8, 31, 1024], P('segment')
- grad_out: float32 [8, 1024, 1024], P('segment', 'dp')
The draws below stay inside these ranges and needn't reach their ends.
Inputs may be any that keep to these rules, and one draw needn't show every extreme that they name: `evict`: for s < 4 the value at tick 0 is at least 3 and the tick 1 value differs from it; for s >= 4 both values are below 3 and differ. `recall`: for s < 4 the value at tick 0 is at least 3; for s >= 4 values are below 3.
All inputs are finite; a program needn't handle non-finite values.
Results may differ from the reference program's by a relative error of at most 0.00014.
Values sent between devices are 32-bit elements; how exact they have to be, the bound alone decides.
A program may use at most 128 MiB of HBM per device.

```python
import jax
import jax.numpy as jnp
from jax import lax

D = 1024
KW = 31
FRAMES = 128
SEQS = 1
TICKS = 2
SLOTS = 3
B = 32
S = 8
N_SEGMENT = 8
N_DP = 32


def draw_evict(key, part):
    key = jax.random.fold_in(key, 11)
    subkeys = jax.random.split(key, 4)
    segment_ids = jnp.arange(N_SEGMENT)
    first_lent = SLOTS + jax.random.randint(subkeys[0], (N_SEGMENT,), 0, SLOTS)
    first_lent = jnp.where(segment_ids == 0, 2 * SLOTS - 1, first_lent)
    second_any = (first_lent + 1 + jax.random.randint(subkeys[1], (N_SEGMENT,), 0, 2 * SLOTS - 1)) % (2 * SLOTS)
    late_first = jax.random.randint(subkeys[2], (N_SEGMENT,), 0, SLOTS)
    late_first = jnp.where(segment_ids == N_SEGMENT - 1, 0, late_first)
    late_second = (late_first + 1 + jax.random.randint(subkeys[3], (N_SEGMENT,), 0, SLOTS - 1)) % SLOTS
    is_early = segment_ids < N_SEGMENT // 2
    first_write = jnp.where(is_early, first_lent, late_first)
    second = jnp.where(is_early, second_any, late_second)
    return jnp.stack([first_write, second], axis=1).astype(jnp.int32)


def draw_recall(key, part):
    key = jax.random.fold_in(key, 23)
    subkeys = jax.random.split(key, 4)
    segment_ids = jnp.arange(N_SEGMENT)
    first_lent = SLOTS + jax.random.randint(subkeys[0], (N_SEGMENT,), 0, SLOTS)
    first_lent = jnp.where(segment_ids == 0, 2 * SLOTS - 1, first_lent)
    second_any = jax.random.randint(subkeys[1], (N_SEGMENT,), 0, 2 * SLOTS)
    late_first = jax.random.randint(subkeys[2], (N_SEGMENT,), 0, SLOTS)
    late_first = jnp.where(segment_ids == N_SEGMENT - 1, 0, late_first)
    late_second = jax.random.randint(subkeys[3], (N_SEGMENT,), 0, SLOTS)
    is_early = segment_ids < N_SEGMENT // 2
    first_read = jnp.where(is_early, first_lent, late_first)
    second = jnp.where(is_early, second_any, late_second)
    return jnp.stack([first_read, second], axis=1).astype(jnp.int32)


def block_scale(stream_key, extent, cuts, smallest, high):
    level, own = 1.0, jax.random.fold_in(stream_key, 6)
    for position, blocks in cuts:
        heights = jnp.exp(jax.random.uniform(jax.random.fold_in(own, position), (blocks,), jnp.float32, smallest / len(cuts), high / len(cuts)))
        level = level * jnp.repeat(heights, extent[position] // blocks).reshape([-1 if axis == position else 1 for axis in range(len(extent))])
    return level


def noise(key, extent, scale, reach, pieces=(), held_as=jnp.bfloat16):
    gain = block_scale(key, extent, pieces, -0.22, 0.18) if pieces else 1.0
    drawn = jax.random.normal(key, extent, jnp.float32) * scale * gain
    return jnp.minimum(jnp.maximum(drawn, -reach), reach).astype(held_as)


def setup_inputs(seed: int = 0) -> dict:
    seeds = jax.random.split(jax.random.key(seed), 12)
    arriving = noise(seeds[0], (S, B, FRAMES, D), 1.0, 6.0, ((0, 8), (1, 32)), jnp.float32)
    entering = noise(seeds[1], (TICKS - 1, B, FRAMES, D), 1.0, 6.0, ((1, 32),), jnp.float32)
    returning = noise(seeds[2], (S, B, FRAMES, D), 1.0, 6.0, ((0, 8), (1, 32)), jnp.float32)
    loss_grad = noise(seeds[3], (TICKS - 1, B, FRAMES, D), 1.0, 6.0, ((1, 32),), jnp.float32)
    kept = noise(seeds[4], (S, SLOTS, B, FRAMES, D), 1.0, 6.0, ((0, 8), (2, 32)), jnp.float32)
    lent = noise(seeds[5], (S, SLOTS, B, FRAMES, D), 1.0, 6.0, ((0, 8), (2, 32)), jnp.float32)
    w_in = noise(seeds[6], (S, D, 2 * D), D ** -0.5, 0.1875, ((0, 8), (1, 32)), jnp.float32)
    kernel = noise(seeds[7], (S, KW, D), KW ** -0.5, 1.0, ((0, 8),), jnp.float32)
    w_out = noise(seeds[8], (S, D, D), D ** -0.5, 0.1875, ((0, 8), (1, 32)), jnp.float32)
    evict = draw_evict(jax.random.fold_in(seeds[11], 71), 0)
    recall = draw_recall(jax.random.fold_in(seeds[11], 71), 0)
    return dict(arriving=arriving, entering=entering, returning=returning, loss_grad=loss_grad, kept=kept, lent=lent, w_in=w_in, kernel=kernel, w_out=w_out, evict=evict, recall=recall)


EPSILON = 1e-05

def normalize(values):
    center = values - lax.optimization_barrier(jnp.mean(values, axis=-1, keepdims=True))
    spread = lax.optimization_barrier(jnp.mean(center * center, axis=-1, keepdims=True))
    return center * lax.rsqrt(spread + EPSILON)

def module(frames_in, w_first, kernel_taps, w_second):
    seq_count, length, feat_width = frames_in.shape
    normed = normalize(frames_in).reshape(seq_count * length, feat_width)
    joined = jnp.dot(normed, w_first, precision=lax.Precision.HIGHEST, preferred_element_type=jnp.float32)
    gated_units = (joined[:, :feat_width] * jax.nn.sigmoid(joined[:, feat_width:])).reshape(seq_count, length, feat_width)
    half_width = kernel_taps.shape[0] // 2
    padded = jnp.pad(gated_units, ((0, 0), (half_width, half_width), (0, 0)))
    mixed_units = padded[:, 0:length] * kernel_taps[0]
    for offset in range(1, kernel_taps.shape[0]):
        mixed_units = mixed_units + padded[:, offset:offset + length] * kernel_taps[offset]
    normal_mix = normalize(mixed_units)
    swished = (normal_mix * jax.nn.sigmoid(normal_mix)).reshape(seq_count * length, feat_width)
    projected = jnp.dot(swished, w_second, precision=lax.Precision.HIGHEST, preferred_element_type=jnp.float32)
    return frames_in + projected.reshape(seq_count, length, feat_width)

def reference(arriving, entering, returning, loss_grad, kept, lent, w_in, kernel, w_out, evict, recall):
    segments = N_SEGMENT
    slot_ids = jnp.arange(SLOTS, dtype=jnp.int32)
    segment_ids = jnp.arange(segments, dtype=jnp.int32)
    kept_now = kept
    lent_now = lent
    sum_first = jnp.zeros(w_in.shape, jnp.float32)
    sum_taps = jnp.zeros(kernel.shape, jnp.float32)
    sum_second = jnp.zeros(w_out.shape, jnp.float32)
    forward_out = arriving
    backward_out = returning
    for tick in range(TICKS):
        if tick == 0:
            fwd_in = arriving
            back_in = returning
        else:
            fwd_in = jnp.concatenate([entering[tick - 1][None], forward_out[:-1]], axis=0)
            back_in = jnp.concatenate([backward_out[1:], loss_grad[tick - 1][None]], axis=0)
        reads = recall[:, tick].astype(jnp.int32)
        own_pick = kept_now[segment_ids, jnp.clip(reads, 0, SLOTS - 1)]
        lent_flip = lent_now[::-1]
        other_pick = lent_flip[segment_ids, jnp.clip(reads - SLOTS, 0, SLOTS - 1)]
        stash = jnp.where((reads < SLOTS)[:, None, None, None], own_pick, other_pick)
        forward_list = []
        backward_list = []
        first_list = []
        taps_list = []
        second_list = []
        for segment in range(segments):
            forward_list.append(module(fwd_in[segment], w_in[segment], kernel[segment], w_out[segment]))
            unused, pullback = jax.vjp(module, stash[segment], w_in[segment], kernel[segment], w_out[segment])
            d_input, d_first, d_taps, d_second = pullback(back_in[segment])
            backward_list.append(d_input)
            first_list.append(d_first)
            taps_list.append(d_taps)
            second_list.append(d_second)
        forward_out = jnp.stack(forward_list)
        backward_out = jnp.stack(backward_list)
        sum_first = sum_first + jnp.stack(first_list)
        sum_taps = sum_taps + jnp.stack(taps_list)
        sum_second = sum_second + jnp.stack(second_list)
        writes = evict[:, tick].astype(jnp.int32)
        keep_mask = slot_ids[None, :] == writes[:, None]
        kept_now = jnp.where(keep_mask[:, :, None, None, None], fwd_in[:, None], kept_now)
        lend_mask = (slot_ids[None, :] + SLOTS == writes[:, None])[::-1]
        lent_now = jnp.where(lend_mask[:, :, None, None, None], fwd_in[::-1][:, None], lent_now)
    scale = float(TICKS * SEQS * N_DP * FRAMES) ** (-0.5)
    return (forward_out, backward_out, kept_now, lent_now, sum_first * scale, sum_taps * scale, sum_second * scale)
```

```python
import jax
import jax.numpy as jnp
from jax import lax
from jax.experimental import pallas as pl
from jax.experimental.pallas import tpu as pltpu
from jax.sharding import PartitionSpec as P

F, D, KW = 128, 1024, 31
IN, OUT, ALL = 2 * D, D, 3 * D
EPSILON = 1e-05
SCALE = float(2 * 32 * F) ** (-0.5)
BF, F32 = jnp.bfloat16, jnp.float32
NN = (((1,), (0,)), ((), ()))
NT = (((1,), (1,)), ((), ()))
MESH = pl.DeviceIdType.MESH
N_SEMS = 160
RING = (2, 1, 3, 0)
ORDER = (
    (2, 2), (1, 2), (3, 2), (0, 2), (2, 1), (2, 3), (2, 0),
    (1, 1), (1, 3), (3, 1), (3, 3), (0, 1), (0, 3), (1, 0), (3, 0), (0, 0),
)


def split(v):
    hi = v.astype(BF)
    return hi, (v - hi.astype(F32)).astype(BF)


def dot3(ah, al, bh, bl, dims):
    def one(a, b):
        return lax.dot_general(a, b, dims, preferred_element_type=F32)

    return one(ah, bh) + (one(ah, bl) + one(al, bh))


def loop(n, step, body):
    def run(i, carry):
        body(pl.multiple_of(i * step, step))
        return carry

    lax.fori_loop(0, n // step, run, 0)


def stats(v):
    center = v - jnp.mean(v, axis=-1, keepdims=True)
    inv = lax.rsqrt(jnp.mean(center * center, axis=-1, keepdims=True) + EPSILON)
    return center * inv, inv


def window(
    sel, arriving, entering, returning, loss, own0, own1, ex0, lend1, w_in, taps, w_out,
    passed, returned, a1_out, x0_out, x1_out, g_in, g_tap, g_out,
    W, Wh, Wl, S, R1, R2, T1, T2, H, Xh, Xl, XN, XTh, XTl, ZTh, ZTl, DHh, DHl, Gh, Gl,
    U0, U1, DC, C, ZN, INV, DZ, ST, YR, DR, V1, X0, X1, TP, DT, TR, send, recv,
):
    z = lax.axis_index("segment")
    d = lax.axis_index("dp")
    x, y, c = d // 8, (d // 2) % 4, d % 2

    def chip(xo, yo):
        return ((x + xo) % 4) * 8 + ((y + yo) % 4) * 2

    def rows_of(xo, yo, core):
        return pl.multiple_of((chip(xo, yo) + core) * 32, 32)

    def slot(xo, yo):
        return pl.multiple_of((chip(xo, yo) // 2) * 32, 32)

    def place(h, po, qo):
        return (po, qo) if h == 0 else (qo, po)

    def near(h, axis, sign):
        along_x = (h == 0) == (axis == 0)
        return {"dp": (chip(sign, 0) if along_x else chip(0, sign)) + c}

    sibling = {"dp": d + 1 - 2 * c}
    above = {"segment": (z + 1) % 8}
    below = {"segment": (z + 7) % 8}
    mirror = {"segment": 7 - z}

    barrier = pltpu.get_barrier_semaphore()
    peers = [near(0, a, s) for a in (0, 1) for s in (1, 3)] + [sibling, above, below, mirror]
    for peer in peers:
        pl.semaphore_signal(barrier, inc=1, device_id=peer, device_id_type=MESH)
    pl.semaphore_wait(barrier, len(peers))

    used = [0]
    sent = []

    def remote(src, dst, device, start=True):
        i = used[0]
        used[0] += 1
        copy = pltpu.make_async_remote_copy(
            src_ref=src, dst_ref=dst, send_sem=send.at[i], recv_sem=recv.at[i],
            device_id=device, device_id_type=MESH,
        )
        if start:
            copy.start()
        sent.append(copy)
        return copy

    copy_x0 = remote(ex0, X0, mirror)
    copy_x1 = remote(V1, X1, mirror, start=False)

    @pl.when(z >= 4)
    def _():
        V1[...] = lend1[...]
        copy_x1.start()

    mine = rows_of(0, 0, c)
    W[pl.ds(mine, 32), :IN] = w_in[...]
    W[pl.ds(mine, 32), IN:] = w_out[...]

    def pass_on(row, n, device):
        part = W.at[pl.ds(pl.multiple_of(row, 8), n), :]
        return remote(part, part, device)

    def piece(h, po, qo):
        return rows_of(*place(h, po, qo), c) + 16 * h

    first = {}
    second = {}
    far = {}
    over = []
    for h in (0, 1):
        for sign in (1, 3):
            first[h, sign] = pass_on(piece(h, 0, 0), 16, near(h, 0, sign))

    def along_q(h, po):
        for sign in (1, 3):
            second[h, po, sign] = pass_on(piece(h, po, 0), 16, near(h, 1, sign))

    for h in (0, 1):
        along_q(h, 0)
    over.append(pass_on(mine, 32, sibling))

    def norm_in(src, row0):
        def body(r):
            v, _ = stats(src[pl.ds(r, 16), :])
            XN[pl.ds(r, 16), :] = v
            hi, lo = split(v)
            Xh[pl.ds(row0 + r, 16), :] = hi
            Xl[pl.ds(row0 + r, 16), :] = lo

        loop(F, 16, body)

    norm_in(arriving, F)
    U0[...] = jnp.zeros_like(U0)
    U1[...] = jnp.zeros_like(U1)
    DC[...] = jnp.zeros_like(DC)
    DT[...] = jnp.zeros_like(DT)

    def cotangent(src, t):
        def body(r):
            hi, lo = split(src[pl.ds(r, 16), :])
            Gh[pl.ds(t * F + r, 16), :] = hi
            Gl[pl.ds(t * F + r, 16), :] = lo

        loop(F, 16, body)

    cotangent(returning, 0)

    ahead = {}
    for sign, back, lower in ((1, 3, 0), (3, 1, 8)):
        for h in (0, 1):
            first[h, sign].wait_recv()
            ahead[h, sign] = pass_on(piece(h, back, 0) + lower, 8, near(h, 0, sign))
            along_q(h, back)
            over.append(pass_on(piece(h, back, 0), 16, sibling))
    for h in (0, 1):
        for sign in (1, 3):
            ahead[h, sign].wait_recv()
        along_q(h, 2)
        over.append(pass_on(piece(h, 2, 0), 16, sibling))
    for po in (0, 3, 1, 2):
        for h in (0, 1):
            for sign, back, lower in ((1, 3, 0), (3, 1, 8)):
                second[h, po, sign].wait_recv()
                far[h, po, sign] = pass_on(piece(h, po, back) + lower, 8, near(h, 1, sign))
                over.append(pass_on(piece(h, po, back), 16, sibling))
    for po in (0, 3, 1, 2):
        for h in (0, 1):
            for sign in (1, 3):
                far[h, po, sign].wait_recv()
            over.append(pass_on(piece(h, po, 2), 16, sibling))
    for copy in over:
        copy.wait_recv()
    for copy in sent[2:]:
        copy.wait_send()
    del sent[2:]

    def halves(r):
        for j in range(3):
            hi, lo = split(W[pl.ds(r, 16), j * D : (j + 1) * D])
            Wh[pl.ds(r, 16), j * D : (j + 1) * D] = hi
            Wl[pl.ds(r, 16), j * D : (j + 1) * D] = lo

    loop(D, 16, halves)

    def project(ah, al, row0, m, col0, n, out):
        def body(j):
            cols = pl.ds(pl.multiple_of(col0 + j, 256), 256)
            out[0:m, pl.ds(j, 256)] = dot3(
                ah[row0 : row0 + m, :], al[row0 : row0 + m, :], Wh[:, cols], Wl[:, cols], NN
            )

        loop(n, 256, body)

    def project_back(ah, al, row0, col0, k, out):
        def body(j):
            out[:, pl.ds(j, 256)] = dot3(
                ah[row0 : row0 + F, :], al[row0 : row0 + F, :],
                Wh[pl.ds(j, 256), col0 : col0 + k], Wl[pl.ds(j, 256), col0 : col0 + k], NT,
            )

        loop(D, 256, body)

    def turn(src, th, tl, t):
        def body(j):
            hi, lo = split(src[:, pl.ds(j, 128)].T)
            th[pl.ds(j, 128), t * F : (t + 1) * F] = hi
            tl[pl.ds(j, 128), t * F : (t + 1) * F] = lo

        loop(D, 128, body)

    def gate_and_mix(row0, u_pad):
        def body(j, carry):
            left = pl.ds(pl.multiple_of(j * 128, 128), 128)
            right = pl.ds(pl.multiple_of(D + j * 128, 128), 128)
            gate = lax.logistic(H[row0 : row0 + F, right])
            H[row0 : row0 + F, right] = gate
            u_pad[j, 16 : 16 + F, :] = H[row0 : row0 + F, left] * gate
            total = u_pad[j, 1 : 1 + F, :] * taps[0:1, left]
            for k in range(1, KW):
                total = total + u_pad[j, 1 + k : 1 + k + F, :] * taps[k : k + 1, left]
            C[:, left] = total
            return carry

        lax.fori_loop(0, 8, body, 0)

    def swish(keep, send_on):
        def body(r):
            zn, inv = stats(C[pl.ds(r, 16), :])
            w = zn * lax.logistic(zn)
            if keep:
                ZN[pl.ds(r, 16), :] = zn
                INV[pl.ds(r, 16), :] = jnp.broadcast_to(inv, (16, 128))
                C[pl.ds(r, 16), :] = w
            if send_on:
                hi, lo = split(w)
                Xh[pl.ds(r, 16), :] = hi
                Xl[pl.ds(r, 16), :] = lo

        loop(F, 16, body)

    def recompute(t, u_pad):
        gate_and_mix(0, u_pad)
        swish(True, False)
        turn(C, ZTh, ZTl, t)

    def add_rows(a, b, out):
        def body(r):
            out[pl.ds(r, 16), :] = a[pl.ds(r, 16), :] + b[pl.ds(r, 16), :]

        loop(F, 16, body)

    def backward(t, u_pad, g, out, between):
        project_back(Gh, Gl, t * F, IN, OUT, DZ)

        def inner(r):
            zn, dw = ZN[pl.ds(r, 16), :], DZ[pl.ds(r, 16), :]
            s = lax.logistic(zn)
            dz = dw * (s * (1.0 + zn * (1.0 - s)))
            both = jnp.mean(dz, axis=-1, keepdims=True)
            slope = jnp.mean(dz * zn, axis=-1, keepdims=True)
            DZ[pl.ds(r, 16), :] = INV[pl.ds(r, 16), 0:1] * (dz - both - zn * slope)

        loop(F, 16, inner)

        def unmix(j, carry):
            left = pl.ds(pl.multiple_of(j * 128, 128), 128)
            right = pl.ds(pl.multiple_of(D + j * 128, 128), 128)
            DC[j, 16 : 16 + F, :] = DZ[:, left]
            du = DC[j, 31 : 31 + F, :] * taps[0:1, left]
            for k in range(1, KW):
                du = du + DC[j, 31 - k : 31 - k + F, :] * taps[k : k + 1, left]
            gate = H[0:F, right]
            hi, lo = split(du * gate)
            DHh[t * F : (t + 1) * F, left] = hi
            DHl[t * F : (t + 1) * F, left] = lo
            hi, lo = split(du * u_pad[j, 16 : 16 + F, :] * (1.0 - gate))
            DHh[t * F : (t + 1) * F, right] = hi
            DHl[t * F : (t + 1) * F, right] = lo
            return carry

        lax.fori_loop(0, 8, unmix, 0)
        between()
        project_back(DHh, DHl, t * F, 0, IN, DZ)

        def outer(r):
            v, inv = stats(ST[pl.ds(r, 16), :])
            dv = DZ[pl.ds(r, 16), :]
            both = jnp.mean(dv, axis=-1, keepdims=True)
            slope = jnp.mean(dv * v, axis=-1, keepdims=True)
            out[pl.ds(r, 16), :] = g[pl.ds(r, 16), :] + inv * (dv - both - v * slope)

        loop(F, 16, outer)

    def tap_grads(t, u_pad):
        def body(j, carry):
            left = pl.ds(pl.multiple_of(j * 128, 128), 128)
            dc = DC[j, 16 : 16 + F, :].reshape(16, 8, 128)
            for k in range(KW):
                part = jnp.sum(dc * u_pad[j, 1 + k : 1 + k + F, :].reshape(16, 8, 128), axis=0)
                if t == 0:
                    TP[j, k] = part
                else:
                    DT[0, k : k + 1, left] = jnp.sum(part + TP[j, k], axis=0, keepdims=True)
            return carry

        lax.fori_loop(0, 8, body, 0)

    copy_x0.wait_recv()

    @pl.when(z < 4)
    def _():
        ST[...] = X0[...]

    @pl.when(z >= 4)
    def _():
        ST[...] = own0[...]

    norm_in(ST, 0)
    turn(XN, XTh, XTl, 0)
    project(Xh, Xl, 0, 2 * F, 0, IN, H)
    recompute(0, U0)
    backward(0, U0, returning, returned, lambda: None)
    copy_d = remote(returned, DR, below)
    tap_grads(0, U0)
    gate_and_mix(F, U1)
    swish(False, True)
    project(Xh, Xl, 0, F, IN, OUT, DZ)
    add_rows(arriving, DZ, passed)
    copy_y = remote(passed, YR, above)

    @pl.when(z < 4)
    def _():
        copy_x1.wait_recv()

        def body(r):
            for j in range(8):
                lanes = slice(j * 128, (j + 1) * 128)
                chosen = jnp.broadcast_to(sel[0:1, :], (16, 128)) > 0
                ST[pl.ds(r, 16), lanes] = jnp.where(
                    chosen, X1[pl.ds(r, 16), lanes], own1[pl.ds(r, 16), lanes]
                )

        loop(F, 16, body)

    @pl.when(z >= 4)
    def _():
        ST[...] = own1[...]

    norm_in(ST, 0)
    turn(XN, XTh, XTl, 1)
    project(Xh, Xl, 0, F, 0, IN, H)
    recompute(1, U1)
    copy_d.wait()

    @pl.when(z == 7)
    def _():
        DR[...] = loss[...]

    cotangent(DR, 1)

    rounds = [0]
    odd_x, odd_y = x % 2, y % 2
    partners = [
        sibling,
        {"dp": chip(1 - 2 * odd_x + 4, 0) + c},
        {"dp": chip(3 + 2 * odd_x, 0) + c},
        {"dp": chip(0, 1 - 2 * odd_y + 4) + c},
        {"dp": chip(0, 3 + 2 * odd_y) + c},
    ]
    tap_copy = [None]

    def tap_round():
        i = rounds[0]
        if i > 0:
            tap_copy[0].wait_recv()
            DT[i] = DT[i - 1] + TR[i - 1]
        if i < 5:
            tap_copy[0] = remote(DT.at[i], TR.at[i], partners[i])
        rounds[0] += 1

    def between():
        tap_grads(1, U1)
        tap_round()

    backward(1, U1, DR, returned, between)
    tap_round()

    def weight_grad(th, tl, dh, dl, cols_in, cols_out):
        def body(r):
            out = dot3(th[pl.ds(r, 256), :], tl[pl.ds(r, 256), :], dh[:, cols_in], dl[:, cols_in], NN)
            W[pl.ds(r, 256), cols_out] = out

        loop(D, 256, body)

    def grad_out(j):
        weight_grad(ZTh, ZTl, Gh, Gl, pl.ds(j, 256), pl.ds(pl.multiple_of(IN + j, 256), 256))

    def grad_in(j):
        weight_grad(XTh, XTl, DHh, DHl, pl.ds(j, 256), pl.ds(j, 256))

    loop(OUT, 256, grad_out)
    tap_round()
    loop(IN, 256, grad_in)
    tap_round()

    pair = {}
    for o in ORDER:
        pair[o] = remote(W.at[pl.ds(rows_of(*o, 1 - c), 32), :], S.at[pl.ds(slot(*o), 32), :], sibling)

    def add_pair(o):
        pair[o].wait_recv()
        base, mine_rows = slot(*o), rows_of(*o, c)

        def body(r):
            S[pl.ds(base + r, 8), :] = S[pl.ds(base + r, 8), :] + W[pl.ds(mine_rows + r, 8), :]

        loop(32, 8, body)

    def part(h, po, qo, lower, n):
        row = slot(*place(h, po, qo)) + 16 * h + lower
        return pl.ds(pl.multiple_of(row, 8), n)

    def add_from(rows, *others):
        total = S[rows, :]
        for other in others:
            total = total + other
        S[rows, :] = total

    m1, m2 = {}, {}

    def open_ring(h, i, po):
        for side, sign in ((0, 1), (1, 3)):
            m1[h, i, side] = remote(
                S.at[part(h, po, 2, 8 * side, 8), :], R1.at[h, side, i], near(h, 1, sign)
            )

    for n, o in enumerate(ORDER):
        add_pair(o)
        if n < 4:
            open_ring(0, n, o[0])
        if n == 0 or 4 <= n < 7:
            open_ring(1, RING.index(o[1]), o[1])
    for i, po in enumerate(RING):
        for h in (0, 1):
            for side, sign in ((0, 1), (1, 3)):
                m1[h, i, side].wait_recv()
                add_from(part(h, po, sign, 8 * side, 8), R1[h, side, i])
                m2[h, i, side] = remote(
                    S.at[part(h, po, sign, 0, 16), :], R2.at[h, side, i], near(h, 1, sign)
                )
    tap_round()

    copy_y.wait()

    @pl.when(z == 0)
    def _():
        YR[...] = entering[...]

    @pl.when(z < 4)
    def _():
        V1[...] = YR[...]
        copy_x1.start()

    norm_in(YR, 0)
    project(Xh, Xl, 0, F, 0, IN, H)
    gate_and_mix(0, U0)
    swish(False, True)
    project(Xh, Xl, 0, F, IN, OUT, DZ)
    add_rows(YR, DZ, passed)
    a1_out[...] = YR[...]
    tap_round()
    g_tap[...] = DT[5, 0:KW, :] * SCALE

    t1, t2 = {}, {}
    for i, po in enumerate(RING):
        for h in (0, 1):
            for side in (0, 1):
                m2[h, i, side].wait_recv()
            add_from(part(h, po, 0, 0, 16), R2[h, 0, i], R2[h, 1, i])
            if i == 0:
                for side, sign in ((0, 1), (1, 3)):
                    t1[h, side] = remote(
                        S.at[part(h, 2, 0, 8 * side, 8), :], T1.at[h, side], near(h, 0, sign)
                    )
    for h in (0, 1):
        for side, sign in ((0, 1), (1, 3)):
            t1[h, side].wait_recv()
            add_from(part(h, sign, 0, 8 * side, 8), T1[h, side])
            t2[h, side] = remote(
                S.at[part(h, sign, 0, 0, 16), :], T2.at[h, side], near(h, 0, sign)
            )
    for h in (0, 1):
        for side in (0, 1):
            t2[h, side].wait_recv()
        total = (S[part(h, 0, 0, 0, 16), :] + T2[h, 0] + T2[h, 1]) * SCALE
        g_in[16 * h : 16 * h + 16, :] = total[:, :IN]
        g_out[16 * h : 16 * h + 16, :] = total[:, IN:]

    @pl.when(z >= 4)
    def _():
        copy_x1.wait_recv()

    x0_out[...] = X0[...]
    x1_out[...] = X1[...]
    done = {id(copy_d), id(copy_y)}
    for copy in sent:
        if id(copy) not in done:
            copy.wait_send()


def run_window(sel, *operands):
    def f32(*shape):
        return jax.ShapeDtypeStruct(shape, F32)

    def vf(*shape):
        return pltpu.VMEM(shape, F32)

    def vb(*shape):
        return pltpu.VMEM(shape, BF)

    row = (F, D)
    vmem = pl.BlockSpec(memory_space=pltpu.VMEM)
    scratch = [
        vf(D, ALL), vb(D, ALL), vb(D, ALL), vf(512, ALL),
        vf(2, 2, 4, 8, ALL), vf(2, 2, 4, 16, ALL), vf(2, 2, 8, ALL), vf(2, 2, 16, ALL),
        vf(2 * F, IN), vb(2 * F, D), vb(2 * F, D), vf(*row),
        vb(D, 2 * F), vb(D, 2 * F), vb(D, 2 * F), vb(D, 2 * F), vb(2 * F, IN), vb(2 * F, IN),
        vb(2 * F, D), vb(2 * F, D),
        vf(8, 160, 128), vf(8, 160, 128), vf(8, 160, 128), vf(*row), vf(*row), vf(F, 128), vf(*row), vf(*row),
        vf(*row), vf(*row), vf(*row), vf(*row), vf(*row),
        vf(8, 32, 8, 128), vf(6, 32, D), vf(5, 32, D),
        pltpu.SemaphoreType.DMA((N_SEMS,)), pltpu.SemaphoreType.DMA((N_SEMS,)),
    ]
    return pl.pallas_call(
        window,
        out_shape=(
            f32(*row), f32(*row), f32(*row), f32(*row), f32(*row), f32(32, IN), f32(KW, D), f32(32, OUT),
        ),
        in_specs=[vmem] * (1 + len(operands)),
        out_specs=(vmem,) * 8,
        scratch_shapes=scratch,
        compiler_params=pltpu.CompilerParams(
            collective_id=0, has_side_effects=True, vmem_limit_bytes=62 * 1024 * 1024
        ),
    )(sel, *operands)


def shards(
    arriving, entering, returning, loss_grad, kept, lent, w_in, kernel, w_out, evict, recall
):
    position = lax.axis_index("segment")
    mirror = 7 - position
    kept_now, lent_now = kept[0, :, 0], lent[0, :, 0]
    arrived = arriving[0, 0]

    def pick(stack, i):
        return lax.dynamic_index_in_dim(stack, jnp.clip(i, 0, 2), 0, keepdims=False)

    read, write = recall[position], evict[position]
    their_read, their_write = recall[mirror], evict[mirror]
    own0 = pick(kept_now, read[0])
    own1 = jnp.where(read[1] == write[0], arrived, pick(kept_now, read[1]))
    lend0 = pick(lent_now, their_read[0] - 3)
    lend1 = pick(lent_now, their_read[1] - 3)
    exchanged = jnp.where(position < 4, arrived, lend0)
    use_lent = jnp.logical_and(read[1] >= 3, read[1] != write[0])
    sel = jnp.broadcast_to(use_lent.astype(jnp.int32), (8, 128))
    passed, returned, a1, x0, x1, g_in, g_tap, g_out = run_window(
        sel, arrived, entering[0, 0], returning[0, 0], loss_grad[0, 0], own0, own1, exchanged, lend1,
        w_in[0], kernel[0], w_out[0],
    )
    slot_ids = jnp.arange(3, dtype=jnp.int32)[:, None, None]
    kept_out = jnp.where(slot_ids == write[0], arrived[None], kept_now)
    kept_out = jnp.where(slot_ids == write[1], a1[None], kept_out)
    lent_out = jnp.where(slot_ids + 3 == their_write[0], x0[None], lent_now)
    lent_out = jnp.where(slot_ids + 3 == their_write[1], x1[None], lent_out)
    return (
        passed[None, None], returned[None, None], kept_out[None, :, None], lent_out[None, :, None],
        g_in[None], g_tap[None], g_out[None],
    )


def solution(mesh):
    placed = (
        P("segment", "dp", None, None),
        P(None, "dp", None, None),
        P("segment", "dp", None, None),
        P(None, "dp", None, None),
        P("segment", None, "dp", None, None),
        P("segment", None, "dp", None, None),
        P("segment", "dp", None),
        P("segment", None, None),
        P("segment", "dp", None),
        P(),
        P(),
    )
    return jax.shard_map(
        shards,
        mesh=mesh,
        in_specs=placed,
        out_specs=(
            P("segment", "dp", None, None),
            P("segment", "dp", None, None),
            P("segment", None, "dp", None, None),
            P("segment", None, "dp", None, None),
            P("segment", "dp", None),
            P("segment", None, None),
            P("segment", "dp", None),
        ),
        check_vma=False,
    )
```

```python
import jax
import jax.numpy as jnp
from jax import lax
from jax.experimental import pallas as pl
from jax.experimental.pallas import tpu as pltpu
from jax.sharding import PartitionSpec as P

F, D, KW = 128, 1024, 31
IN, OUT, ALL = 2 * D, D, 3 * D
EPSILON = 1e-05
SCALE = float(2 * 32 * F) ** (-0.5)
BF, F32 = jnp.bfloat16, jnp.float32
NN = (((1,), (0,)), ((), ()))
NT = (((1,), (1,)), ((), ()))
MESH = pl.DeviceIdType.MESH
N_SEMS = 288
RING = (2, 1, 3, 0)
SIDES = ((0, 1, 3), (1, 3, 1))
RB = 64


def split(v):
    hi = v.astype(BF)
    return hi, (v - hi.astype(F32)).astype(BF)


def dot3(ah, al, bh, bl, dims):
    def one(a, b):
        return lax.dot_general(a, b, dims, preferred_element_type=F32)

    return one(ah, bh) + (one(ah, bl) + one(al, bh))


def loop(n, step, body, unroll=1):
    def run(i, carry):
        body(pl.multiple_of(i * step, step))
        return carry

    lax.fori_loop(0, n // step, run, 0, unroll=unroll)


def stats(v):
    center = v - jnp.mean(v, axis=-1, keepdims=True)
    inv = lax.rsqrt(jnp.mean(center * center, axis=-1, keepdims=True) + EPSILON)
    return center * inv, inv


def window(
    evict, recall, arriving, entering, returning, loss, kept, lent, w_in, taps, w_out,
    passed, returned, a1_out, x0_out, x1_out, g_in, g_tap, g_out,
    W, Wh, Wl, S, R1, R2, T1, T2, H, Xh, Xl, XN, XTh, XTl, ZTh, ZTl, DHh, DHl, Gh, Gl,
    U0, U1, DC, C, ZN, INV, DZ, ST, YR, DR, V0, V1, X0, X1, A, B, EDGE, PB, QB, TP, DT, TR,
    send, recv, local, free,
):
    z = lax.axis_index("segment")
    d = lax.axis_index("dp")
    x, y, c = d // 8, (d // 2) % 4, d % 2

    def chip(xo, yo):
        return ((x + xo) % 4) * 4 + ((y + yo) % 4)

    def place(h, po, qo):
        return (po, qo) if h == 0 else (qo, po)

    def near(h, axis, sign):
        along_x = (h == 0) == (axis == 0)
        return {"dp": (chip(sign, 0) if along_x else chip(0, sign)) * 2 + c}

    sibling = {"dp": d + 1 - 2 * c}
    above = {"segment": (z + 1) % 8}
    below = {"segment": (z + 7) % 8}
    mirror = {"segment": 7 - z}

    def fetch(i, src, dst):
        copy = pltpu.make_async_copy(src, dst, local.at[i])
        copy.start()
        return copy

    here = chip(0, 0)
    get_lent = fetch(3, lent, S.at[0:12, :, D : 2 * D])
    get_in = fetch(0, w_in, W.at[here, c, :, 0:IN])
    get_a = fetch(2, arriving, A)
    get_kept = fetch(5, kept, S.at[0:12, :, 0:D])
    get_out = fetch(1, w_out, W.at[here, c, :, IN:ALL])
    get_b = fetch(4, returning, B)

    @pl.when(z == 0)
    def _():
        fetch(6, entering, EDGE)

    @pl.when(z == 7)
    def _():
        fetch(6, loss, EDGE)

    barrier = pltpu.get_barrier_semaphore()
    peers = [near(0, a, s) for a in (0, 1) for s in (1, 3)] + [sibling, above, below, mirror]
    for peer in peers:
        pl.semaphore_signal(barrier, inc=1, device_id=peer, device_id_type=MESH)
    pl.semaphore_wait(barrier, len(peers))

    used = [0]
    sent = []

    def remote(src, dst, device, start=True):
        i = used[0]
        used[0] += 1
        copy = pltpu.make_async_remote_copy(
            src_ref=src, dst_ref=dst, send_sem=send.at[i], recv_sem=recv.at[i],
            device_id=device, device_id_type=MESH,
        )
        if start:
            copy.start()
        sent.append(copy)
        return copy

    def settle():
        for copy in sent:
            copy.wait_send()
        sent.clear()

    class Gather:
        def __init__(self, cols):
            self.cols = cols
            self.first, self.second, self.ahead, self.far, self.over = {}, {}, {}, {}, {}

        def pass_on(self, xo, yo, row, n, device):
            part = W.at[chip(xo, yo), c, row : row + n, self.cols]
            return remote(part, part, device)

        def piece(self, h, po, qo, device, lower=0, n=16):
            return self.pass_on(*place(h, po, qo), 16 * h + lower, n, device)

        def along_q(self, h, po):
            for sign in (1, 3):
                self.second[h, po, sign] = self.piece(h, po, 0, near(h, 1, sign))

        def cross(self, h, po, qo):
            self.over[h, po, qo] = self.piece(h, po, qo, sibling)

        def start(self):
            for h in (0, 1):
                for sign in (1, 3):
                    self.first[h, sign] = self.piece(h, 0, 0, near(h, 0, sign))
            for h in (0, 1):
                self.along_q(h, 0)
                self.cross(h, 0, 0)

        def one(self):
            for side, sign, back in SIDES:
                for h in (0, 1):
                    self.first[h, sign].wait_recv()
                    self.ahead[h, sign] = self.piece(h, back, 0, near(h, 0, sign), 8 * side, 8)
                    self.along_q(h, back)
                    self.cross(h, back, 0)

        def two(self):
            for h in (0, 1):
                for sign in (1, 3):
                    self.ahead[h, sign].wait_recv()
                self.along_q(h, 2)
                self.cross(h, 2, 0)

        def three(self, order):
            for po in order:
                for h in (0, 1):
                    for side, sign, back in SIDES:
                        self.second[h, po, sign].wait_recv()
                        self.far[h, po, sign] = self.piece(h, po, back, near(h, 1, sign), 8 * side, 8)
                        self.cross(h, po, back)

        def halve(self, h, po, core):
            for qo in range(4):
                i = chip(*place(h, po, qo))
                row = pl.multiple_of(i * 64 + core * 32 + 16 * h, 16)
                hi, lo = split(W[i, core, 16 * h : 16 * h + 16, self.cols])
                Wh[pl.ds(row, 16), self.cols] = hi
                Wl[pl.ds(row, 16), self.cols] = lo

        def four(self, order):
            for po in order:
                for h in (0, 1):
                    for sign in (1, 3):
                        self.far[h, po, sign].wait_recv()
                    self.cross(h, po, 2)
                    self.halve(h, po, c)

        def five(self, order):
            for po in order:
                for h in (0, 1):
                    for qo in range(4):
                        self.over[h, po, qo].wait_recv()
                    self.halve(h, po, 1 - c)

    first_in, first_out = Gather(slice(0, IN)), Gather(slice(IN, ALL))
    get_in.wait()
    first_in.start()

    get_lent.wait()
    get_a.wait()
    get_kept.wait()
    theirs = 7 - z

    def lent_slot(t):
        return S[pl.ds(4 * jnp.clip(recall[theirs, t] - 3, 0, 2), 4), :, D : 2 * D].reshape(F, D)

    @pl.when(z < 4)
    def _():
        V0[...] = A[...]

    @pl.when(z >= 4)
    def _():
        V0[...] = lent_slot(0)
        V1[...] = lent_slot(1)

    copy_x0 = remote(V0, X0, mirror)
    copy_x1 = remote(V1, X1, mirror, start=False)
    sent.pop()

    def norm_in(src, row0):
        def body(r):
            v, _ = stats(src[pl.ds(r, RB), :])
            XN[pl.ds(r, RB), :] = v
            hi, lo = split(v)
            Xh[pl.ds(row0 + r, RB), :] = hi
            Xl[pl.ds(row0 + r, RB), :] = lo

        loop(F, RB, body)

    def cotangent(src, t):
        def body(r):
            hi, lo = split(src[pl.ds(r, RB), :])
            Gh[pl.ds(t * F + r, RB), :] = hi
            Gl[pl.ds(t * F + r, RB), :] = lo

        loop(F, RB, body)

    def turn(src, th, tl, t):
        def body(j):
            hi, lo = split(src[:, pl.ds(j, 128)].T)
            th[pl.ds(j, 128), t * F : (t + 1) * F] = hi
            tl[pl.ds(j, 128), t * F : (t + 1) * F] = lo

        loop(D, 128, body, 2)

    first_in.one()
    norm_in(A, F)
    first_in.two()
    for pad in (U0, U1, DC):
        pad[:, 0:16, :] = jnp.zeros((8, 16, 128), F32)
        pad[:, 16 + F :, :] = jnp.zeros((8, 16, 128), F32)
    DT[0, 248:256, :] = jnp.zeros((8, 128), F32)
    get_b.wait()
    cotangent(B, 0)
    order = (0, 3, 1, 2)
    first_in.three(order)
    get_out.wait()
    first_out.start()
    first_in.four(order[:3])
    first_out.one()
    copy_x0.wait_recv()

    @pl.when(z >= 4)
    def _():
        copy_x1.start()

    @pl.when(z < 4)
    def _():
        ST[...] = X0[...]

    @pl.when(z >= 4)
    def _():
        ST[...] = S[pl.ds(4 * jnp.clip(recall[z, 0], 0, 2), 4), :, 0:D].reshape(F, D)

    norm_in(ST, 0)
    first_in.four(order[3:])
    first_out.two()
    first_in.five(order)
    first_out.three(order[:1])

    def project(ah, al, row0, m, col0, n, out, unroll=2):
        def body(j):
            cols = pl.ds(pl.multiple_of(col0 + j, 256), 256)
            out[0:m, pl.ds(j, 256)] = dot3(
                ah[row0 : row0 + m, :], al[row0 : row0 + m, :], Wh[:, cols], Wl[:, cols], NN
            )

        loop(n, 256, body, unroll)

    def project_back(ah, al, row0, col0, k, out, unroll=2):
        def body(j):
            out[:, pl.ds(j, 256)] = dot3(
                ah[row0 : row0 + F, :], al[row0 : row0 + F, :],
                Wh[pl.ds(j, 256), col0 : col0 + k], Wl[pl.ds(j, 256), col0 : col0 + k], NT,
            )

        loop(D, 256, body, unroll)

    def gate_and_mix(row0, u_pad):
        def body(j, carry):
            left = pl.ds(pl.multiple_of(j * 128, 128), 128)
            right = pl.ds(pl.multiple_of(D + j * 128, 128), 128)
            gate = lax.logistic(H[row0 : row0 + F, right])
            H[row0 : row0 + F, right] = gate
            u_pad[j, 16 : 16 + F, :] = H[row0 : row0 + F, left] * gate
            total = u_pad[j, 1 : 1 + F, :] * taps[pl.ds(j, 1), :]
            for k in range(1, KW):
                total = total + u_pad[j, 1 + k : 1 + k + F, :] * taps[pl.ds(8 * k + j, 1), :]
            C[:, left] = total
            return carry

        lax.fori_loop(0, 8, body, 0)

    def swish(keep, send_on):
        def body(r):
            zn, inv = stats(C[pl.ds(r, RB), :])
            w = zn * lax.logistic(zn)
            if keep:
                ZN[pl.ds(r, RB), :] = zn
                INV[pl.ds(r, RB), :] = jnp.broadcast_to(inv, (RB, 128))
                C[pl.ds(r, RB), :] = w
            if send_on:
                hi, lo = split(w)
                Xh[pl.ds(r, RB), :] = hi
                Xl[pl.ds(r, RB), :] = lo

        loop(F, RB, body)

    def add_rows(a, b, out):
        def body(r):
            out[pl.ds(r, RB), :] = a[pl.ds(r, RB), :] + b[pl.ds(r, RB), :]

        loop(F, RB, body)

    def unswish():
        def body(r):
            zn, dw = ZN[pl.ds(r, RB), :], DZ[pl.ds(r, RB), :]
            s = lax.logistic(zn)
            dz = dw * (s * (1.0 + zn * (1.0 - s)))
            both = jnp.mean(dz, axis=-1, keepdims=True)
            slope = jnp.mean(dz * zn, axis=-1, keepdims=True)
            DZ[pl.ds(r, RB), :] = INV[pl.ds(r, RB), 0:1] * (dz - both - zn * slope)

        loop(F, RB, body)

    def unmix(t, u_pad):
        def body(j, carry):
            left = pl.ds(pl.multiple_of(j * 128, 128), 128)
            right = pl.ds(pl.multiple_of(D + j * 128, 128), 128)
            DC[j, 16 : 16 + F, :] = DZ[:, left]
            du = DC[j, 31 : 31 + F, :] * taps[pl.ds(j, 1), :]
            for k in range(1, KW):
                du = du + DC[j, 31 - k : 31 - k + F, :] * taps[pl.ds(8 * k + j, 1), :]
            gate = H[0:F, right]
            hi, lo = split(du * gate)
            DHh[t * F : (t + 1) * F, left] = hi
            DHl[t * F : (t + 1) * F, left] = lo
            hi, lo = split(du * u_pad[j, 16 : 16 + F, :] * (1.0 - gate))
            DHh[t * F : (t + 1) * F, right] = hi
            DHl[t * F : (t + 1) * F, right] = lo
            return carry

        lax.fori_loop(0, 8, body, 0)

    def input_cotangent(g, out):
        def body(r):
            v, inv = stats(ST[pl.ds(r, RB), :])
            dv = DZ[pl.ds(r, RB), :]
            both = jnp.mean(dv, axis=-1, keepdims=True)
            slope = jnp.mean(dv * v, axis=-1, keepdims=True)
            out[pl.ds(r, RB), :] = g[pl.ds(r, RB), :] + inv * (dv - both - v * slope)

        loop(F, RB, body)

    def tap_grads(t, u_pad):
        def body(j, carry):
            dc = DC[j, 16 : 16 + F, :].reshape(16, 8, 128)
            for k in range(KW):
                part = jnp.sum(dc * u_pad[j, 1 + k : 1 + k + F, :].reshape(16, 8, 128), axis=0)
                if t == 0:
                    TP[j, k] = part
                else:
                    DT[0, pl.ds(8 * k + j, 1), :] = jnp.sum(part + TP[j, k], axis=0, keepdims=True)
            return carry

        lax.fori_loop(0, 8, body, 0)

    project(Xh, Xl, 0, 2 * F, 0, IN, H)
    first_out.three(order[1:])
    turn(XN, XTh, XTl, 0)
    gate_and_mix(0, U0)
    swish(True, False)
    turn(C, ZTh, ZTl, 0)
    first_out.four(order)
    gate_and_mix(F, U1)
    swish(False, True)
    first_out.five(order)
    project_back(Gh, Gl, 0, IN, OUT, DZ)
    unswish()
    unmix(0, U0)
    project_back(DHh, DHl, 0, 0, IN, DZ)
    input_cotangent(B, QB)
    copy_d = remote(QB, DR, below)
    project(Xh, Xl, 0, F, IN, OUT, DZ)
    add_rows(A, DZ, PB)
    copy_y = remote(PB, YR, above)
    tap_grads(0, U0)

    @pl.when(z < 4)
    def _():
        copy_x1.wait_recv()

    use_own = (recall[z, 1] == evict[z, 0]).astype(jnp.int32)
    use_lent = (recall[z, 1] >= 3).astype(jnp.int32)
    slot1 = 4 * jnp.clip(recall[z, 1], 0, 2)

    def choose(r):
        own = jnp.broadcast_to(use_own, (32, D)) > 0
        away = jnp.broadcast_to(use_lent, (32, D)) > 0
        value = S[slot1 + r // 32, :, 0:D]
        value = jnp.where(away, X1[pl.ds(r, 32), :], value)
        ST[pl.ds(r, 32), :] = jnp.where(own, A[pl.ds(r, 32), :], value)

    def choose_own(r):
        own = jnp.broadcast_to(use_own, (32, D)) > 0
        ST[pl.ds(r, 32), :] = jnp.where(own, A[pl.ds(r, 32), :], S[slot1 + r // 32, :, 0:D])

    @pl.when(z < 4)
    def _():
        loop(F, 32, choose)

    @pl.when(z >= 4)
    def _():
        loop(F, 32, choose_own)

    pl.semaphore_signal(free, inc=1, device_id=sibling, device_id_type=MESH)
    norm_in(ST, 0)
    turn(XN, XTh, XTl, 1)
    project(Xh, Xl, 0, F, 0, IN, H)
    gate_and_mix(0, U1)
    swish(True, False)
    turn(C, ZTh, ZTl, 1)

    @pl.when(jnp.logical_or(z == 0, z == 7))
    def _():
        pltpu.make_async_copy(loss, EDGE, local.at[6]).wait()

    copy_d.wait_recv()
    settle()

    @pl.when(z == 7)
    def _():
        DR[...] = EDGE[...]

    cotangent(DR, 1)

    odd_x, odd_y = x % 2, y % 2
    partners = [
        sibling,
        {"dp": chip(5 - 2 * odd_x, 0) * 2 + c},
        {"dp": chip(3 + 2 * odd_x, 0) * 2 + c},
        {"dp": chip(0, 5 - 2 * odd_y) * 2 + c},
        {"dp": chip(0, 3 + 2 * odd_y) * 2 + c},
    ]
    tap_copy = []

    def tap_round():
        i = len(tap_copy)
        if i > 0:
            tap_copy[-1].wait_recv()
            DT[i] = DT[i - 1] + TR[i - 1]
        if i < 5:
            tap_copy.append(remote(DT.at[i], TR.at[i], partners[i]))

    def weight_grad(th, tl, dh, dl, cols_in, cols_out):
        out = dot3(th[...], tl[...], dh[:, cols_in], dl[:, cols_in], NN)
        W[:, :, :, cols_out] = out.reshape(16, 2, 32, 256)

    def grad_out(j):
        weight_grad(ZTh, ZTl, Gh, Gl, pl.ds(j, 256), pl.ds(pl.multiple_of(IN + j, 256), 256))

    def grad_in(base):
        def body(j):
            cols = pl.ds(pl.multiple_of(base + j, 256), 256)
            weight_grad(XTh, XTl, DHh, DHl, cols, cols)

        loop(D, 256, body)

    class Reduce:
        def __init__(self, col0, out, out0):
            self.cols = slice(col0, col0 + D)
            self.out, self.out_cols = out, slice(out0, out0 + D)
            self.pair, self.m1, self.m2, self.t1, self.t2 = {}, {}, {}, {}, {}

        def start(self):
            for xo in RING:
                group = pl.ds(((x + xo) % 4) * 4, 4)
                self.pair[xo] = remote(
                    W.at[group, 1 - c, :, self.cols], S.at[group, :, self.cols], sibling
                )

        def at(self, h, po, qo, lower, n):
            return S.at[chip(*place(h, po, qo)), 16 * h + lower : 16 * h + lower + n, self.cols]

        def add(self, h, po, qo, lower, n, *others):
            i, rows = chip(*place(h, po, qo)), slice(16 * h + lower, 16 * h + lower + n)
            total = S[i, rows, self.cols]
            for other in others:
                total = total + other
            S[i, rows, self.cols] = total

        def open(self, h, i):
            for side, sign, _ in SIDES:
                self.m1[h, i, side] = remote(
                    self.at(h, RING[i], 2, 8 * side, 8), R1.at[h, side, i, :, self.cols], near(h, 1, sign)
                )

        def pairs(self):
            for n, xo in enumerate(RING):
                self.pair[xo].wait_recv()
                base = ((x + xo) % 4) * 4

                def body(i, carry):
                    S[base + i, :, self.cols] = S[base + i, :, self.cols] + W[base + i, c, :, self.cols]
                    return carry

                lax.fori_loop(0, 4, body, 0)
                self.open(0, n)
                if n == 0:
                    for i in range(4):
                        self.open(1, i)

        def middle(self):
            for i, po in enumerate(RING):
                for h in (0, 1):
                    for side, sign, _ in SIDES:
                        self.m1[h, i, side].wait_recv()
                        self.add(h, po, sign, 8 * side, 8, R1[h, side, i, :, self.cols])
                        self.m2[h, i, side] = remote(
                            self.at(h, po, sign, 0, 16), R2.at[h, side, i, :, self.cols], near(h, 1, sign)
                        )

        def turn(self):
            for i, po in enumerate(RING):
                for h in (0, 1):
                    for side in (0, 1):
                        self.m2[h, i, side].wait_recv()
                    self.add(h, po, 0, 0, 16, R2[h, 0, i, :, self.cols], R2[h, 1, i, :, self.cols])
                    if i == 0:
                        for side, sign, _ in SIDES:
                            self.t1[h, side] = remote(
                                self.at(h, 2, 0, 8 * side, 8), T1.at[h, side, :, self.cols], near(h, 0, sign)
                            )

        def last(self):
            for h in (0, 1):
                for side, sign, _ in SIDES:
                    self.t1[h, side].wait_recv()
                    self.add(h, sign, 0, 8 * side, 8, T1[h, side, :, self.cols])
                    self.t2[h, side] = remote(
                        self.at(h, sign, 0, 0, 16), T2.at[h, side, :, self.cols], near(h, 0, sign)
                    )

        def finish(self):
            for h in (0, 1):
                for side in (0, 1):
                    self.t2[h, side].wait_recv()
                rows = slice(16 * h, 16 * h + 16)
                total = S[chip(0, 0), rows, self.cols]
                for side in (0, 1):
                    total = total + T2[h, side, :, self.cols]
                self.out[rows, self.out_cols] = total * SCALE

    sum_out, sum_left, sum_right = Reduce(IN, g_out, 0), Reduce(0, g_in, 0), Reduce(D, g_in, D)
    loop(OUT, 256, grad_out)
    pl.semaphore_wait(free, 1)
    sum_out.start()
    project_back(Gh, Gl, F, IN, OUT, DZ)
    sum_out.pairs()
    unswish()
    unmix(1, U1)
    sum_out.middle()
    grad_in(0)
    sum_left.start()
    tap_grads(1, U1)
    tap_round()
    grad_in(D)
    sum_right.start()
    sum_left.pairs()
    tap_round()
    sum_out.turn()
    sum_left.middle()
    sum_right.pairs()
    project_back(DHh, DHl, F, 0, IN, DZ)
    tap_round()
    sum_out.last()
    sum_right.middle()
    input_cotangent(DR, QB)
    put_q = fetch(0, QB, returned)

    copy_y.wait_recv()

    @pl.when(z == 0)
    def _():
        YR[...] = EDGE[...]

    @pl.when(z < 4)
    def _():
        V1[...] = YR[...]
        copy_x1.start()

    put_a = fetch(1, YR, a1_out)
    norm_in(YR, 0)
    tap_round()
    sum_out.finish()
    sum_left.turn()
    project(Xh, Xl, 0, F, 0, IN, H)
    sum_left.last()
    tap_round()
    gate_and_mix(0, U0)
    swish(False, True)
    project(Xh, Xl, 0, F, IN, OUT, DZ)
    add_rows(YR, DZ, PB)
    put_p = fetch(2, PB, passed)
    put_x0 = fetch(3, X0, x0_out)
    tap_round()
    g_tap[...] = DT[5, 0 : 8 * KW, :] * SCALE
    sum_right.turn()
    sum_left.finish()
    sum_right.last()

    @pl.when(z >= 4)
    def _():
        copy_x1.wait_recv()

    put_x1 = fetch(4, X1, x1_out)
    sum_right.finish()
    copy_x1.wait_send()
    settle()
    for put in (put_q, put_a, put_p, put_x0, put_x1):
        put.wait()


def run_window(*operands):
    def f32(*shape):
        return jax.ShapeDtypeStruct(shape, F32)

    def vf(*shape):
        return pltpu.VMEM(shape, F32)

    def vb(*shape):
        return pltpu.VMEM(shape, BF)

    row = (F, D)
    vmem, smem = pl.BlockSpec(memory_space=pltpu.VMEM), pl.BlockSpec(memory_space=pltpu.SMEM)
    hbm = pl.BlockSpec(memory_space=pl.ANY)
    scratch = [
        vf(16, 2, 32, ALL), vb(D, ALL), vb(D, ALL), vf(16, 32, ALL),
        vf(2, 2, 4, 8, ALL), vf(2, 2, 4, 16, ALL), vf(2, 2, 8, ALL), vf(2, 2, 16, ALL),
        vf(2 * F, IN), vb(2 * F, D), vb(2 * F, D), vf(*row),
        vb(D, 2 * F), vb(D, 2 * F), vb(D, 2 * F), vb(D, 2 * F), vb(2 * F, IN), vb(2 * F, IN),
        vb(2 * F, D), vb(2 * F, D),
        vf(8, 160, 128), vf(8, 160, 128), vf(8, 160, 128), vf(*row), vf(*row), vf(F, 128), vf(*row), vf(*row),
        vf(*row), vf(*row), vf(*row), vf(*row), vf(*row), vf(*row), vf(*row), vf(*row), vf(*row), vf(*row), vf(*row),
        vf(8, 32, 8, 128), vf(6, 256, 128), vf(5, 256, 128),
        pltpu.SemaphoreType.DMA((N_SEMS,)), pltpu.SemaphoreType.DMA((N_SEMS,)), pltpu.SemaphoreType.DMA((8,)),
        pltpu.SemaphoreType.REGULAR,
    ]
    return pl.pallas_call(
        window,
        out_shape=(
            f32(*row), f32(*row), f32(*row), f32(*row), f32(*row), f32(32, IN), f32(8 * KW, 128), f32(32, OUT),
        ),
        in_specs=[smem] * 2 + [hbm] * 7 + [vmem, hbm],
        out_specs=(hbm,) * 5 + (vmem,) * 3,
        scratch_shapes=scratch,
        compiler_params=pltpu.CompilerParams(
            collective_id=0, has_side_effects=True, vmem_limit_bytes=63 * 1024 * 1024
        ),
    )(*operands)


def deliver(
    evict, kept, lent, arriving, a1, x0, x1, passed, returned, g_in, g_tap, g_out,
    o_passed, o_returned, o_kept, o_lent, o_in, o_tap, o_out,
    v_passed, v_returned, v_kept, v_lent, v_in, v_tap, v_out, sems,
):
    z = lax.axis_index("segment")
    plain = (
        (passed, v_passed, o_passed), (returned, v_returned, o_returned),
        (g_in, v_in, o_in), (g_tap, v_tap, o_tap), (g_out, v_out, o_out),
    )
    moves = []
    for src, held, dst in plain:
        copy = pltpu.make_async_copy(src, held, sems.at[0, len(moves)])
        copy.start()
        moves.append((copy, held, dst))
    for section, base, before, held, out, early, late in (
        (z, 0, kept, v_kept, o_kept, arriving, a1),
        (7 - z, 3, lent, v_lent, o_lent, x0, x1),
    ):
        for i in range(3):
            is_early = evict[section, 0] == base + i
            is_late = evict[section, 1] == base + i
            sem = sems.at[0, len(moves)]

            @pl.when(is_late)
            def _():
                pltpu.make_async_copy(late, held.at[i], sem).start()

            @pl.when(jnp.logical_and(is_early, jnp.logical_not(is_late)))
            def _():
                pltpu.make_async_copy(early, held.at[i], sem).start()

            @pl.when(jnp.logical_not(jnp.logical_or(is_early, is_late)))
            def _():
                pltpu.make_async_copy(before.at[i], held.at[i], sem).start()

            moves.append((pltpu.make_async_copy(before.at[i], held.at[i], sem), held.at[i], out.at[i]))
    leaving = []
    for i, (copy, held, dst) in enumerate(moves):
        copy.wait()
        copy = pltpu.make_async_copy(held, dst, sems.at[1, i])
        copy.start()
        leaving.append(copy)
    for copy in leaving:
        copy.wait()


def run_deliver(*operands):
    shapes = ((F, D), (F, D), (3, F, D), (3, F, D), (32, IN), (8 * KW, 128), (32, OUT))
    hbm = pl.BlockSpec(memory_space=pl.ANY)
    return pl.pallas_call(
        deliver,
        out_shape=tuple(jax.ShapeDtypeStruct(shape, F32) for shape in shapes),
        in_specs=[pl.BlockSpec(memory_space=pltpu.SMEM)] + [hbm] * 11,
        out_specs=(hbm,) * 7,
        scratch_shapes=[pltpu.VMEM(shape, F32) for shape in shapes] + [pltpu.SemaphoreType.DMA((2, 11))],
    )(*operands)


def shards(
    arriving, entering, returning, loss_grad, kept, lent, w_in, kernel, w_out, evict, recall
):
    arrived = arriving[0, 0]
    kept_now, lent_now = kept[0, :, 0], lent[0, :, 0]
    passed, returned, a1, x0, x1, g_in, g_tap, g_out = run_window(
        evict, recall, arrived, entering[0, 0], returning[0, 0], loss_grad[0, 0],
        kept_now.reshape(12, 32, D), lent_now.reshape(12, 32, D), w_in[0], kernel.reshape(8 * KW, 128), w_out[0],
    )
    passed, returned, kept_out, lent_out, g_in, g_tap, g_out = run_deliver(
        evict, kept_now, lent_now, arrived, a1, x0, x1, passed, returned, g_in, g_tap, g_out
    )
    return (
        passed[None, None], returned[None, None], kept_out[None, :, None], lent_out[None, :, None],
        g_in[None], g_tap.reshape(1, KW, D), g_out[None],
    )


def solution(mesh):
    placed = (
        P("segment", "dp", None, None),
        P(None, "dp", None, None),
        P("segment", "dp", None, None),
        P(None, "dp", None, None),
        P("segment", None, "dp", None, None),
        P("segment", None, "dp", None, None),
        P("segment", "dp", None),
        P("segment", None, None),
        P("segment", "dp", None),
        P(),
        P(),
    )
    return jax.shard_map(
        shards,
        mesh=mesh,
        in_specs=placed,
        out_specs=(
            P("segment", "dp", None, None),
            P("segment", "dp", None, None),
            P("segment", None, "dp", None, None),
            P("segment", None, "dp", None, None),
            P("segment", "dp", None),
            P("segment", None, None),
            P("segment", "dp", None),
        ),
        check_vma=False,
    )
```

```python
import jax
import jax.numpy as jnp
from jax import lax
from jax.experimental import pallas as pl
from jax.experimental.pallas import tpu as pltpu
from jax.sharding import PartitionSpec as P

F, D, KW = 128, 1024, 31
IN, OUT, ALL = 2 * D, D, 3 * D
EPSILON = 1e-05
SCALE = float(2 * 32 * F) ** (-0.5)
BF, F32 = jnp.bfloat16, jnp.float32
NN = (((1,), (0,)), ((), ()))
NT = (((1,), (1,)), ((), ()))
MESH = pl.DeviceIdType.MESH
N_SEMS = 288
RING = (2, 1, 3, 0)
SIDES = ((0, 1, 3), (1, 3, 1))
RB = 64
LEFT = 1024


def split(v):
    hi = v.astype(BF)
    return hi, (v - hi.astype(F32)).astype(BF)


def dot3(ah, al, bh, bl, dims):
    def one(a, b):
        return lax.dot_general(a, b, dims, preferred_element_type=F32)

    return one(ah, bh) + (one(ah, bl) + one(al, bh))


def loop(n, step, body, unroll=1):
    def run(i, carry):
        body(pl.multiple_of(i * step, step))
        return carry

    lax.fori_loop(0, n // step, run, 0, unroll=unroll)


def stats(v):
    center = v - jnp.mean(v, axis=-1, keepdims=True)
    inv = lax.rsqrt(jnp.mean(center * center, axis=-1, keepdims=True) + EPSILON)
    return center * inv, inv


def window(
    slots, arriving, entering, returning, loss, kept, lent, w_in, taps, w_out,
    passed, returned, a1_out, x0_out, x1_out, g_in, g_tap, g_out,
    W, Wh, Wl, S, R1, R2, T1, T2, H, Xh, Xl, XN, XTh, XTl, ZTh, ZTl, DHh, DHl, Gh, Gl,
    U0, U1, DC, C, ZN, INV, DZ, ST, YR, DR, V0, V1, X0, X1, A, B, EDGE, PB, QB, TP, DT, TR,
    send, recv, local, free,
):
    z = lax.axis_index("segment")
    d = lax.axis_index("dp")
    x, y, c = d // 8, (d // 2) % 4, d % 2

    def chip(xo, yo):
        return ((x + xo) % 4) * 4 + ((y + yo) % 4)

    def place(h, po, qo):
        return (po, qo) if h == 0 else (qo, po)

    def near(h, axis, sign):
        along_x = (h == 0) == (axis == 0)
        return {"dp": (chip(sign, 0) if along_x else chip(0, sign)) * 2 + c}

    sibling = {"dp": d + 1 - 2 * c}
    above = {"segment": (z + 1) % 8}
    below = {"segment": (z + 7) % 8}
    mirror = {"segment": 7 - z}

    def fetch(i, src, dst):
        copy = pltpu.make_async_copy(src, dst, local.at[i])
        copy.start()
        return copy

    here = chip(0, 0)
    get_lent = fetch(3, lent, S.at[0:12, :, D : 2 * D])
    get_in = fetch(0, w_in, W.at[here, c, :, 0:IN])
    get_a = fetch(2, arriving, A)
    get_kept = fetch(5, kept, S.at[0:12, :, 0:D])
    get_out = fetch(1, w_out, W.at[here, c, :, IN:ALL])
    get_b = fetch(4, returning, B)

    @pl.when(z == 0)
    def _():
        fetch(6, entering, EDGE)

    @pl.when(z == 7)
    def _():
        fetch(6, loss, EDGE)

    barrier = pltpu.get_barrier_semaphore()
    peers = [near(0, a, s) for a in (0, 1) for s in (1, 3)] + [sibling, above, below, mirror]
    for peer in peers:
        pl.semaphore_signal(barrier, inc=1, device_id=peer, device_id_type=MESH)
    pl.semaphore_wait(barrier, len(peers))

    used = [0]
    sent = []

    def remote(src, dst, device, start=True):
        i = used[0]
        used[0] += 1
        copy = pltpu.make_async_remote_copy(
            src_ref=src, dst_ref=dst, send_sem=send.at[i], recv_sem=recv.at[i],
            device_id=device, device_id_type=MESH,
        )
        if start:
            copy.start()
        sent.append(copy)
        return copy

    def settle():
        for copy in sent:
            copy.wait_send()
        sent.clear()

    class Gather:
        def __init__(self, cols):
            self.cols = cols
            self.first, self.second, self.ahead, self.far, self.over = {}, {}, {}, {}, {}

        def pass_on(self, xo, yo, row, n, device):
            part = W.at[chip(xo, yo), c, row : row + n, self.cols]
            return remote(part, part, device)

        def piece(self, h, po, qo, device, lower=0, n=16):
            return self.pass_on(*place(h, po, qo), 16 * h + lower, n, device)

        def along_q(self, h, po):
            for sign in (1, 3):
                self.second[h, po, sign] = self.piece(h, po, 0, near(h, 1, sign))

        def cross(self, h, po, qo):
            self.over[h, po, qo] = self.piece(h, po, qo, sibling)

        def start(self):
            for h in (0, 1):
                for sign in (1, 3):
                    self.first[h, sign] = self.piece(h, 0, 0, near(h, 0, sign))
            for h in (0, 1):
                self.along_q(h, 0)
                self.cross(h, 0, 0)

        def one(self):
            for side, sign, back in SIDES:
                for h in (0, 1):
                    self.first[h, sign].wait_recv()
                    self.ahead[h, sign] = self.piece(h, back, 0, near(h, 0, sign), 8 * side, 8)
                    self.along_q(h, back)
                    self.cross(h, back, 0)

        def two(self):
            for h in (0, 1):
                for sign in (1, 3):
                    self.ahead[h, sign].wait_recv()
                self.along_q(h, 2)
                self.cross(h, 2, 0)

        def three(self, order):
            for po in order:
                for h in (0, 1):
                    for side, sign, back in SIDES:
                        self.second[h, po, sign].wait_recv()
                        self.far[h, po, sign] = self.piece(h, po, back, near(h, 1, sign), 8 * side, 8)
                        self.cross(h, po, back)

        def halve(self, h, po, core):
            for qo in range(4):
                i = chip(*place(h, po, qo))
                row = pl.multiple_of(i * 64 + core * 32 + 16 * h, 16)
                hi, lo = split(W[i, core, 16 * h : 16 * h + 16, self.cols])
                Wh[pl.ds(row, 16), self.cols] = hi
                Wl[pl.ds(row, 16), self.cols] = lo

        def four(self, order):
            for po in order:
                for h in (0, 1):
                    for sign in (1, 3):
                        self.far[h, po, sign].wait_recv()
                    self.cross(h, po, 2)
                    self.halve(h, po, c)

        def five(self, order):
            for po in order:
                for h in (0, 1):
                    for qo in range(4):
                        self.over[h, po, qo].wait_recv()
                    self.halve(h, po, 1 - c)

    first_in, first_out = Gather(slice(0, IN)), Gather(slice(IN, ALL))
    get_in.wait()
    first_in.start()

    get_lent.wait()
    get_a.wait()
    get_kept.wait()
    theirs = 7 - z

    def lent_slot(t):
        return S[pl.ds(4 * jnp.clip(slots[4 * theirs + 2 + t] - 3, 0, 2), 4), :, D : 2 * D].reshape(F, D)

    @pl.when(z < 4)
    def _():
        V0[...] = A[...]

    @pl.when(z >= 4)
    def _():
        V0[...] = lent_slot(0)
        V1[...] = lent_slot(1)

    copy_x0 = remote(V0, X0, mirror)
    copy_x1 = remote(V1, X1, mirror, start=False)
    sent.pop()

    def norm_in(src, row0):
        def body(r):
            v, _ = stats(src[pl.ds(r, RB), :])
            XN[pl.ds(r, RB), :] = v
            hi, lo = split(v)
            Xh[pl.ds(row0 + r, RB), :] = hi
            Xl[pl.ds(row0 + r, RB), :] = lo

        loop(F, RB, body)

    def cotangent(src, t):
        def body(r):
            hi, lo = split(src[pl.ds(r, RB), :])
            Gh[pl.ds(t * F + r, RB), :] = hi
            Gl[pl.ds(t * F + r, RB), :] = lo

        loop(F, RB, body)

    def turn(src, th, tl, t):
        def body(j):
            hi, lo = split(src[:, pl.ds(j, 128)].T)
            th[pl.ds(j, 128), t * F : (t + 1) * F] = hi
            tl[pl.ds(j, 128), t * F : (t + 1) * F] = lo

        loop(D, 128, body, 2)

    first_in.one()
    norm_in(A, F)
    first_in.two()
    for pad in (U0, U1, DC):
        pad[:, 0:16, :] = jnp.zeros((8, 16, 128), F32)
        pad[:, 16 + F :, :] = jnp.zeros((8, 16, 128), F32)
    DT[0, 248:256, :] = jnp.zeros((8, 128), F32)
    get_b.wait()
    cotangent(B, 0)
    order = (0, 3, 1, 2)
    first_in.three(order)
    get_out.wait()
    first_out.start()
    first_in.four(order[:3])
    first_out.one()
    copy_x0.wait_recv()

    @pl.when(z >= 4)
    def _():
        copy_x1.start()

    @pl.when(z < 4)
    def _():
        ST[...] = X0[...]

    @pl.when(z >= 4)
    def _():
        ST[...] = S[pl.ds(4 * jnp.clip(slots[4 * z + 2], 0, 2), 4), :, 0:D].reshape(F, D)

    norm_in(ST, 0)
    first_in.four(order[3:])
    first_out.two()
    first_in.five(order)
    first_out.three(order[:1])

    def project(ah, al, row0, m, col0, n, out, start=0, unroll=2):
        def body(j):
            j = pl.multiple_of(start + j, 256)
            cols = pl.ds(pl.multiple_of(col0 + j, 256), 256)
            out[0:m, pl.ds(j, 256)] = dot3(
                ah[row0 : row0 + m, :], al[row0 : row0 + m, :], Wh[:, cols], Wl[:, cols], NN
            )

        loop(n - start, 256, body, unroll)

    def project_back(ah, al, row0, col0, k, out, start=0, stop=D, unroll=2):
        def body(j):
            j = pl.multiple_of(start + j, 256)
            out[:, pl.ds(j, 256)] = dot3(
                ah[row0 : row0 + F, :], al[row0 : row0 + F, :],
                Wh[pl.ds(j, 256), col0 : col0 + k], Wl[pl.ds(j, 256), col0 : col0 + k], NT,
            )

        loop(stop - start, 256, body, unroll)

    def gate_and_mix(row0, u_pad):
        def body(j, carry):
            left = pl.ds(pl.multiple_of(j * 128, 128), 128)
            right = pl.ds(pl.multiple_of(D + j * 128, 128), 128)
            gate = lax.logistic(H[row0 : row0 + F, right])
            H[row0 : row0 + F, right] = gate
            u_pad[j, 16 : 16 + F, :] = H[row0 : row0 + F, left] * gate
            total = u_pad[j, 1 : 1 + F, :] * taps[pl.ds(j, 1), :]
            for k in range(1, KW):
                total = total + u_pad[j, 1 + k : 1 + k + F, :] * taps[pl.ds(8 * k + j, 1), :]
            C[:, left] = total
            return carry

        lax.fori_loop(0, 8, body, 0)

    def swish(keep, send_on):
        def body(r):
            zn, inv = stats(C[pl.ds(r, RB), :])
            w = zn * lax.logistic(zn)
            if keep:
                ZN[pl.ds(r, RB), :] = zn
                INV[pl.ds(r, RB), :] = jnp.broadcast_to(inv, (RB, 128))
                C[pl.ds(r, RB), :] = w
            if send_on:
                hi, lo = split(w)
                Xh[pl.ds(r, RB), :] = hi
                Xl[pl.ds(r, RB), :] = lo

        loop(F, RB, body)

    def add_rows(a, b, out):
        def body(r):
            out[pl.ds(r, RB), :] = a[pl.ds(r, RB), :] + b[pl.ds(r, RB), :]

        loop(F, RB, body)

    def unswish():
        def body(r):
            zn, dw = ZN[pl.ds(r, RB), :], DZ[pl.ds(r, RB), :]
            s = lax.logistic(zn)
            dz = dw * (s * (1.0 + zn * (1.0 - s)))
            both = jnp.mean(dz, axis=-1, keepdims=True)
            slope = jnp.mean(dz * zn, axis=-1, keepdims=True)
            DZ[pl.ds(r, RB), :] = INV[pl.ds(r, RB), 0:1] * (dz - both - zn * slope)

        loop(F, RB, body)

    def unmix(t, u_pad):
        def body(j, carry):
            left = pl.ds(pl.multiple_of(j * 128, 128), 128)
            right = pl.ds(pl.multiple_of(D + j * 128, 128), 128)
            DC[j, 16 : 16 + F, :] = DZ[:, left]
            du = DC[j, 31 : 31 + F, :] * taps[pl.ds(j, 1), :]
            for k in range(1, KW):
                du = du + DC[j, 31 - k : 31 - k + F, :] * taps[pl.ds(8 * k + j, 1), :]
            gate = H[0:F, right]
            hi, lo = split(du * gate)
            DHh[t * F : (t + 1) * F, left] = hi
            DHl[t * F : (t + 1) * F, left] = lo
            hi, lo = split(du * u_pad[j, 16 : 16 + F, :] * (1.0 - gate))
            DHh[t * F : (t + 1) * F, right] = hi
            DHl[t * F : (t + 1) * F, right] = lo
            return carry

        lax.fori_loop(0, 8, body, 0)

    def input_cotangent(g, out):
        def body(r):
            v, inv = stats(ST[pl.ds(r, RB), :])
            dv = DZ[pl.ds(r, RB), :]
            both = jnp.mean(dv, axis=-1, keepdims=True)
            slope = jnp.mean(dv * v, axis=-1, keepdims=True)
            out[pl.ds(r, RB), :] = g[pl.ds(r, RB), :] + inv * (dv - both - v * slope)

        loop(F, RB, body)

    def tap_grads(t, u_pad):
        def body(j, carry):
            dc = DC[j, 16 : 16 + F, :].reshape(16, 8, 128)
            for k in range(KW):
                part = jnp.sum(dc * u_pad[j, 1 + k : 1 + k + F, :].reshape(16, 8, 128), axis=0)
                if t == 0:
                    TP[j, k] = part
                else:
                    DT[0, pl.ds(8 * k + j, 1), :] = jnp.sum(part + TP[j, k], axis=0, keepdims=True)
            return carry

        lax.fori_loop(0, 8, body, 0)

    project(Xh, Xl, 0, 2 * F, 0, IN, H)
    first_out.three(order[1:])
    turn(XN, XTh, XTl, 0)
    gate_and_mix(0, U0)
    swish(True, False)
    turn(C, ZTh, ZTl, 0)
    first_out.four(order)
    gate_and_mix(F, U1)
    swish(False, True)
    first_out.five(order)
    project_back(Gh, Gl, 0, IN, OUT, DZ)
    unswish()
    unmix(0, U0)
    project_back(DHh, DHl, 0, 0, IN, DZ)
    input_cotangent(B, QB)
    copy_d = remote(QB, DR, below)
    project(Xh, Xl, 0, F, IN, OUT, DZ)
    add_rows(A, DZ, PB)
    copy_y = remote(PB, YR, above)
    tap_grads(0, U0)

    @pl.when(z < 4)
    def _():
        copy_x1.wait_recv()

    use_own = (slots[4 * z + 3] == slots[4 * z]).astype(jnp.int32)
    use_lent = (slots[4 * z + 3] >= 3).astype(jnp.int32)
    slot1 = 4 * jnp.clip(slots[4 * z + 3], 0, 2)

    def choose(r):
        own = jnp.broadcast_to(use_own, (32, D)) > 0
        away = jnp.broadcast_to(use_lent, (32, D)) > 0
        value = S[slot1 + r // 32, :, 0:D]
        value = jnp.where(away, X1[pl.ds(r, 32), :], value)
        ST[pl.ds(r, 32), :] = jnp.where(own, A[pl.ds(r, 32), :], value)

    def choose_own(r):
        own = jnp.broadcast_to(use_own, (32, D)) > 0
        ST[pl.ds(r, 32), :] = jnp.where(own, A[pl.ds(r, 32), :], S[slot1 + r // 32, :, 0:D])

    @pl.when(z < 4)
    def _():
        loop(F, 32, choose)

    @pl.when(z >= 4)
    def _():
        loop(F, 32, choose_own)

    pl.semaphore_signal(free, inc=1, device_id=sibling, device_id_type=MESH)
    norm_in(ST, 0)
    turn(XN, XTh, XTl, 1)
    project(Xh, Xl, 0, F, 0, IN, H)
    gate_and_mix(0, U1)
    swish(True, False)
    turn(C, ZTh, ZTl, 1)

    @pl.when(jnp.logical_or(z == 0, z == 7))
    def _():
        pltpu.make_async_copy(loss, EDGE, local.at[6]).wait()

    copy_d.wait_recv()
    settle()

    @pl.when(z == 7)
    def _():
        DR[...] = EDGE[...]

    cotangent(DR, 1)

    odd_x, odd_y = x % 2, y % 2
    partners = [
        sibling,
        {"dp": chip(5 - 2 * odd_x, 0) * 2 + c},
        {"dp": chip(3 + 2 * odd_x, 0) * 2 + c},
        {"dp": chip(0, 5 - 2 * odd_y) * 2 + c},
        {"dp": chip(0, 3 + 2 * odd_y) * 2 + c},
    ]
    tap_copy = []

    def tap_round():
        i = len(tap_copy)
        if i > 0:
            tap_copy[-1].wait_recv()
            DT[i] = DT[i - 1] + TR[i - 1]
        if i < 5:
            tap_copy.append(remote(DT.at[i], TR.at[i], partners[i]))

    def weight_grad(th, tl, dh, dl, cols_in, cols_out):
        out = dot3(th[...], tl[...], dh[:, cols_in], dl[:, cols_in], NN)
        W[:, :, :, cols_out] = out.reshape(16, 2, 32, 256)

    def grad_out(j):
        weight_grad(ZTh, ZTl, Gh, Gl, pl.ds(j, 256), pl.ds(pl.multiple_of(IN + j, 256), 256))

    def grad_in(start, stop):
        def body(j):
            cols = pl.ds(pl.multiple_of(start + j, 256), 256)
            weight_grad(XTh, XTl, DHh, DHl, cols, cols)

        loop(stop - start, 256, body)

    class Reduce:
        def __init__(self, col0, width, out, out0):
            self.cols = slice(col0, col0 + width)
            self.out, self.out_cols = out, slice(out0, out0 + width)
            self.pair, self.m1, self.m2, self.t1, self.t2 = {}, {}, {}, {}, {}

        def start(self):
            for xo in RING:
                group = pl.ds(((x + xo) % 4) * 4, 4)
                self.pair[xo] = remote(
                    W.at[group, 1 - c, :, self.cols], S.at[group, :, self.cols], sibling
                )

        def at(self, h, po, qo, lower, n):
            return S.at[chip(*place(h, po, qo)), 16 * h + lower : 16 * h + lower + n, self.cols]

        def add(self, h, po, qo, lower, n, *others):
            i, rows = chip(*place(h, po, qo)), slice(16 * h + lower, 16 * h + lower + n)
            total = S[i, rows, self.cols]
            for other in others:
                total = total + other
            S[i, rows, self.cols] = total

        def open(self, h, i):
            for side, sign, _ in SIDES:
                self.m1[h, i, side] = remote(
                    self.at(h, RING[i], 2, 8 * side, 8), R1.at[h, side, i, :, self.cols], near(h, 1, sign)
                )

        def pairs(self):
            for n, xo in enumerate(RING):
                self.pair[xo].wait_recv()
                base = ((x + xo) % 4) * 4

                def body(i, carry):
                    S[base + i, :, self.cols] = S[base + i, :, self.cols] + W[base + i, c, :, self.cols]
                    return carry

                lax.fori_loop(0, 4, body, 0)
                self.open(0, n)
                if n == 0:
                    for i in range(4):
                        self.open(1, i)

        def middle(self):
            for i, po in enumerate(RING):
                for h in (0, 1):
                    for side, sign, _ in SIDES:
                        self.m1[h, i, side].wait_recv()
                        self.add(h, po, sign, 8 * side, 8, R1[h, side, i, :, self.cols])
                        self.m2[h, i, side] = remote(
                            self.at(h, po, sign, 0, 16), R2.at[h, side, i, :, self.cols], near(h, 1, sign)
                        )

        def turn(self):
            for i, po in enumerate(RING):
                for h in (0, 1):
                    for side in (0, 1):
                        self.m2[h, i, side].wait_recv()
                    self.add(h, po, 0, 0, 16, R2[h, 0, i, :, self.cols], R2[h, 1, i, :, self.cols])
                    if i == 0:
                        for side, sign, _ in SIDES:
                            self.t1[h, side] = remote(
                                self.at(h, 2, 0, 8 * side, 8), T1.at[h, side, :, self.cols], near(h, 0, sign)
                            )

        def last(self):
            for h in (0, 1):
                for side, sign, _ in SIDES:
                    self.t1[h, side].wait_recv()
                    self.add(h, sign, 0, 8 * side, 8, T1[h, side, :, self.cols])
                    self.t2[h, side] = remote(
                        self.at(h, sign, 0, 0, 16), T2.at[h, side, :, self.cols], near(h, 0, sign)
                    )

        def finish(self):
            for h in (0, 1):
                for side in (0, 1):
                    self.t2[h, side].wait_recv()
                rows = slice(16 * h, 16 * h + 16)
                total = S[chip(0, 0), rows, self.cols]
                for side in (0, 1):
                    total = total + T2[h, side, :, self.cols]
                self.out[rows, self.out_cols] = total * SCALE

    sum_out, sum_left = Reduce(IN, OUT, g_out, 0), Reduce(0, LEFT, g_in, 0)
    sum_right = Reduce(LEFT, IN - LEFT, g_in, LEFT)
    half = LEFT // 2
    loop(OUT, 256, grad_out)
    pl.semaphore_wait(free, 1)
    sum_out.start()
    project_back(Gh, Gl, F, IN, OUT, DZ)
    unswish()
    sum_out.pairs()
    unmix(1, U1)
    tap_grads(1, U1)
    tap_round()
    grad_in(0, half)
    tap_round()
    sum_out.middle()
    grad_in(half, LEFT)
    sum_left.start()
    tap_round()
    grad_in(LEFT, LEFT + 512)
    sum_left.pairs()
    grad_in(LEFT + 512, IN)
    sum_right.start()
    sum_out.turn()
    tap_round()
    sum_right.pairs()
    sum_left.middle()
    project_back(DHh, DHl, F, 0, IN, DZ, 0, 512)
    sum_out.last()
    sum_right.middle()
    project_back(DHh, DHl, F, 0, IN, DZ, 512, D)
    tap_round()
    sum_left.turn()
    input_cotangent(DR, QB)
    put_q = fetch(0, QB, returned)

    copy_y.wait_recv()

    @pl.when(z == 0)
    def _():
        YR[...] = EDGE[...]

    @pl.when(z < 4)
    def _():
        V1[...] = YR[...]
        copy_x1.start()

    put_a = fetch(1, YR, a1_out)
    norm_in(YR, 0)
    project(Xh, Xl, 0, F, 0, IN - 1024, H)
    sum_left.last()
    sum_out.finish()
    project(Xh, Xl, 0, F, 0, IN, H, 1024)
    gate_and_mix(0, U0)
    sum_right.turn()
    swish(False, True)
    tap_round()
    project(Xh, Xl, 0, F, IN, OUT, DZ)
    sum_right.last()
    add_rows(YR, DZ, PB)
    put_p = fetch(2, PB, passed)
    put_x0 = fetch(3, X0, x0_out)
    g_tap[...] = DT[5, 0 : 8 * KW, :] * SCALE
    sum_left.finish()

    @pl.when(z >= 4)
    def _():
        copy_x1.wait_recv()

    put_x1 = fetch(4, X1, x1_out)
    sum_right.finish()
    copy_x1.wait_send()
    settle()
    for put in (put_q, put_a, put_p, put_x0, put_x1):
        put.wait()


def run_window(*operands):
    def f32(*shape):
        return jax.ShapeDtypeStruct(shape, F32)

    def vf(*shape):
        return pltpu.VMEM(shape, F32)

    def vb(*shape):
        return pltpu.VMEM(shape, BF)

    row = (F, D)
    vmem, smem = pl.BlockSpec(memory_space=pltpu.VMEM), pl.BlockSpec(memory_space=pltpu.SMEM)
    hbm = pl.BlockSpec(memory_space=pl.ANY)
    scratch = [
        vf(16, 2, 32, ALL), vb(D, ALL), vb(D, ALL), vf(16, 32, ALL),
        vf(2, 2, 4, 8, ALL), vf(2, 2, 4, 16, ALL), vf(2, 2, 8, ALL), vf(2, 2, 16, ALL),
        vf(2 * F, IN), vb(2 * F, D), vb(2 * F, D), vf(*row),
        vb(D, 2 * F), vb(D, 2 * F), vb(D, 2 * F), vb(D, 2 * F), vb(2 * F, IN), vb(2 * F, IN),
        vb(2 * F, D), vb(2 * F, D),
        vf(8, 160, 128), vf(8, 160, 128), vf(8, 160, 128), vf(*row), vf(*row), vf(F, 128), vf(*row), vf(*row),
        vf(*row), vf(*row), vf(*row), vf(*row), vf(*row), vf(*row), vf(*row), vf(*row), vf(*row), vf(*row), vf(*row),
        vf(8, 32, 8, 128), vf(6, 256, 128), vf(5, 256, 128),
        pltpu.SemaphoreType.DMA((N_SEMS,)), pltpu.SemaphoreType.DMA((N_SEMS,)), pltpu.SemaphoreType.DMA((8,)),
        pltpu.SemaphoreType.REGULAR,
    ]
    return pl.pallas_call(
        window,
        out_shape=(
            f32(*row), f32(*row), f32(*row), f32(*row), f32(*row), f32(32, IN), f32(8 * KW, 128), f32(32, OUT),
        ),
        in_specs=[smem] + [hbm] * 7 + [vmem, hbm],
        out_specs=(hbm,) * 5 + (vmem,) * 3,
        scratch_shapes=scratch,
        compiler_params=pltpu.CompilerParams(
            collective_id=0, has_side_effects=True, vmem_limit_bytes=63 * 1024 * 1024
        ),
    )(*operands)


def deliver(
    slots, kept, lent, arriving, a1, x0, x1, passed, returned, g_in, g_tap, g_out,
    o_passed, o_returned, o_kept, o_lent, o_in, o_tap, o_out,
    v_passed, v_returned, v_kept, v_lent, v_in, v_tap, v_out, sems,
):
    z = lax.axis_index("segment")
    plain = (
        (passed, v_passed, o_passed), (returned, v_returned, o_returned),
        (g_in, v_in, o_in), (g_tap, v_tap, o_tap), (g_out, v_out, o_out),
    )
    moves = []
    for src, held, dst in plain:
        copy = pltpu.make_async_copy(src, held, sems.at[0, len(moves)])
        copy.start()
        moves.append((copy, held, dst))
    for section, base, before, held, out, early, late in (
        (z, 0, kept, v_kept, o_kept, arriving, a1),
        (7 - z, 3, lent, v_lent, o_lent, x0, x1),
    ):
        for i in range(3):
            is_early = slots[4 * section] == base + i
            is_late = slots[4 * section + 1] == base + i
            sem = sems.at[0, len(moves)]

            @pl.when(is_late)
            def _():
                pltpu.make_async_copy(late, held.at[i], sem).start()

            @pl.when(jnp.logical_and(is_early, jnp.logical_not(is_late)))
            def _():
                pltpu.make_async_copy(early, held.at[i], sem).start()

            @pl.when(jnp.logical_not(jnp.logical_or(is_early, is_late)))
            def _():
                pltpu.make_async_copy(before.at[i], held.at[i], sem).start()

            moves.append((pltpu.make_async_copy(before.at[i], held.at[i], sem), held.at[i], out.at[i]))
    leaving = []
    for i, (copy, held, dst) in enumerate(moves):
        copy.wait()
        copy = pltpu.make_async_copy(held, dst, sems.at[1, i])
        copy.start()
        leaving.append(copy)
    for copy in leaving:
        copy.wait()


def run_deliver(*operands):
    shapes = ((F, D), (F, D), (3, F, D), (3, F, D), (32, IN), (8 * KW, 128), (32, OUT))
    hbm = pl.BlockSpec(memory_space=pl.ANY)
    return pl.pallas_call(
        deliver,
        out_shape=tuple(jax.ShapeDtypeStruct(shape, F32) for shape in shapes),
        in_specs=[pl.BlockSpec(memory_space=pltpu.SMEM)] + [hbm] * 11,
        out_specs=(hbm,) * 7,
        scratch_shapes=[pltpu.VMEM(shape, F32) for shape in shapes] + [pltpu.SemaphoreType.DMA((2, 11))],
    )(*operands)


def shards(
    arriving, entering, returning, loss_grad, kept, lent, w_in, kernel, w_out, evict, recall
):
    arrived = arriving[0, 0]
    slots = jnp.concatenate([evict, recall], axis=1).reshape(32)
    kept_now, lent_now = kept[0, :, 0], lent[0, :, 0]
    passed, returned, a1, x0, x1, g_in, g_tap, g_out = run_window(
        slots, arrived, entering[0, 0], returning[0, 0], loss_grad[0, 0],
        kept_now.reshape(12, 32, D), lent_now.reshape(12, 32, D), w_in[0], kernel.reshape(8 * KW, 128), w_out[0],
    )
    passed, returned, kept_out, lent_out, g_in, g_tap, g_out = run_deliver(
        slots, kept_now, lent_now, arrived, a1, x0, x1, passed, returned, g_in, g_tap, g_out
    )
    return (
        passed[None, None], returned[None, None], kept_out[None, :, None], lent_out[None, :, None],
        g_in[None], g_tap.reshape(1, KW, D), g_out[None],
    )


def solution(mesh):
    placed = (
        P("segment", "dp", None, None),
        P(None, "dp", None, None),
        P("segment", "dp", None, None),
        P(None, "dp", None, None),
        P("segment", None, "dp", None, None),
        P("segment", None, "dp", None, None),
        P("segment", "dp", None),
        P("segment", None, None),
        P("segment", "dp", None),
        P(),
        P(),
    )
    return jax.shard_map(
        shards,
        mesh=mesh,
        in_specs=placed,
        out_specs=(
            P("segment", "dp", None, None),
            P("segment", "dp", None, None),
            P("segment", None, "dp", None, None),
            P("segment", None, "dp", None, None),
            P("segment", "dp", None),
            P("segment", None, None),
            P("segment", "dp", None),
        ),
        check_vma=False,
    )
```
